32 devices in a mesh: row: 8 (over y, x, core), col: 4 (over z).
Axes of the slice: x: 2, y: 2, z: 4, core: 2. Of those that a mesh axis runs over, the one named last changes fastest.
Arguments:
- cotangent: bfloat16 [2, 256, 8192], P(None, 'row', 'col')
- hidden: bfloat16 [2, 256, 26624], P(None, 'col', 'row')
- context: bfloat16 [2, 256, 8192], P(None, 'col', 'row')
- down_weight: bfloat16 [26624, 8192], P('row', 'col'), may hold values from -0.0390625 to 0.0390625
- heads_weight: bfloat16 [8192, 8192], P('row', 'col'), may hold values from -0.0625 to 0.0625
- spans: int32 [2, 2], replicated, may hold values from 0 to 256, as said below
Outputs:
- down_grad: float32 [26624, 8192], P('row', 'col')
- heads_grad: float32 [8192, 8192], P('row', 'col')
- hidden_grad: bfloat16 [2, 256, 26624], P(None, 'col', 'row')
- context_grad: bfloat16 [2, 256, 8192], P(None, 'col', 'row')
The draws below stay inside these ranges and needn't reach their ends.
Inputs may be any that keep to these rules, and one draw needn't show every extreme that they name: spans[b, 0] is below 64 and spans[b, 1] is 128 or more; some example starts at 0 and some example ends at 256.
All inputs are finite; a program needn't handle non-finite values.
Results may differ from the reference program's by a relative error of at most 0.001.
Values may be sent and summed in bfloat16 or wider, within the bound.
No kernel may reach another device: no remote copies, remote signals or barrier semaphores. Data moves between devices by JAX's collectives and lax.ppermute only.
A program may use at most 256 MiB of HBM per device.

```python
import math
import jax
import jax.numpy as jnp
from jax import lax

DW = 8192
FF_W = 26624
EXAMPLE_COUNT = 2
HD = 8192
SEQ = 256
N_COL = 4


def scaled_field(key, columns, rise):
    first_key = jax.random.fold_in(key, 0)
    fourth_key = jax.random.fold_in(key, 3)
    fifth_key = jax.random.fold_in(key, 4)
    normal_part = jax.random.normal(first_key, (EXAMPLE_COUNT, SEQ, columns), jnp.float32)
    base = normal_part
    row_scale_factor = jnp.exp(jax.random.uniform(fourth_key, (EXAMPLE_COUNT, SEQ, 1), jnp.float32, math.log(0.3), math.log(3.0)))
    position = jnp.arange(columns, dtype=jnp.float32) / columns - 0.5
    column_scale = jnp.exp(jax.random.uniform(fifth_key, (columns,), jnp.float32, math.log(0.3), math.log(3.0)))
    column_scale = column_scale * jnp.exp(math.log(rise) * position)
    return base * row_scale_factor * column_scale


def draw_cotangent(key, part):
    key = jax.random.fold_in(key, 3)
    return scaled_field(key, DW, 3.0).astype(jnp.bfloat16)


def draw_hidden(key, part):
    key = jax.random.fold_in(key, 5)
    return scaled_field(key, FF_W, 3.0).astype(jnp.bfloat16)


def draw_context(key, part):
    key = jax.random.fold_in(key, 9)
    return scaled_field(key, HD, 3.0).astype(jnp.bfloat16)


def draw_spans(key, part):
    key = jax.random.fold_in(key, 7)
    start_key, end_key, full_key, open_key = jax.random.split(key, 4)
    starts = jax.random.randint(start_key, (EXAMPLE_COUNT,), 0, SEQ // 4)
    finish = jax.random.randint(end_key, (EXAMPLE_COUNT,), SEQ // 2, SEQ + 1)
    example_ids = jnp.arange(EXAMPLE_COUNT, dtype=jnp.int32)
    finish = jnp.where(example_ids == jax.random.randint(full_key, (), 0, EXAMPLE_COUNT), SEQ, finish)
    starts = jnp.where(example_ids == jax.random.randint(open_key, (), 0, EXAMPLE_COUNT), 0, starts)
    return jnp.stack([starts, finish], axis=1).astype(jnp.int32)


def shard_levels(stream_key, extent, cuts, low, largest):
    factor_of = 1.0
    for dim, parts in cuts:
        draws = jax.random.uniform(jax.random.fold_in(jax.random.fold_in(stream_key, 6), dim), (parts,), jnp.float32, low / len(cuts), largest / len(cuts))
        factor_of = factor_of * jnp.repeat(jnp.exp(draws), extent[dim] // parts).reshape((-1,) + (1,) * (len(extent) - 1 - dim))
    return factor_of


def bell_draw(stream_key, dims, spread, limit, cuts=(), kind=jnp.bfloat16):
    array = jax.random.normal(stream_key, dims, jnp.float32) * spread
    if len(cuts) > 0:
        array = shard_levels(stream_key, dims, cuts, -0.22, 0.18) * array
    return jnp.clip(array, min=-limit, max=limit).astype(kind)


def setup_inputs(seed: int = 0) -> dict:
    keys = jax.random.split(jax.random.key(seed), 7)
    cotangent = draw_cotangent(jax.random.fold_in(keys[6], 71), 0)
    hidden = draw_hidden(jax.random.fold_in(keys[6], 71), 0)
    context = draw_context(jax.random.fold_in(keys[6], 71), 0)
    down_weight = bell_draw(keys[3], (FF_W, DW), FF_W ** -0.5, 0.0390625, ((0, 8), (1, 4)))
    heads_weight = bell_draw(keys[4], (HD, DW), HD ** -0.5, 0.0625, ((0, 8), (1, 4)))
    spans = draw_spans(jax.random.fold_in(keys[6], 71), 0)
    return {"cotangent": cotangent, "hidden": hidden, "context": context, "down_weight": down_weight, "heads_weight": heads_weight, "spans": spans}


GAMMA = 0.01

def masked_cotangent(cotangent, spans):
    position = jnp.arange(SEQ, dtype=jnp.int32)[None, :]
    keep_mask = ((position >= spans[:, 0:1]) & (position < spans[:, 1:2])).astype(jnp.int32)
    return cotangent * keep_mask[:, :, None].astype(cotangent.dtype)

def ghost_norm(feature_values, masked_values):
    left_gram = jnp.dot(feature_values, feature_values.T, preferred_element_type=jnp.float32)
    right_gram_matrix = jnp.dot(masked_values, masked_values.T, preferred_element_type=jnp.float32)
    return jnp.sum(left_gram * right_gram_matrix)

def clipped_sum(feature_values, masked_values, clip_factor, factor):
    columns = masked_values.shape[2]
    blocks = masked_values.reshape(EXAMPLE_COUNT, SEQ, N_COL, columns // N_COL)
    blocks = jnp.moveaxis(blocks, 2, 0)

    def one_block(column_block):
        running = jnp.zeros((feature_values.shape[2], column_block.shape[2]), jnp.float32)
        for example in range(EXAMPLE_COUNT):
            running = running + clip_factor[example] * jnp.dot(feature_values[example].T, column_block[example], preferred_element_type=jnp.float32)
        return running
    pieces = lax.map(one_block, blocks)
    return factor * jnp.moveaxis(pieces, 0, 1).reshape(feature_values.shape[2], columns)

def input_grad(masked_values, weight):
    rows_list = []
    for example in range(EXAMPLE_COUNT):
        rows_list.append(jnp.dot(masked_values[example], weight.T, preferred_element_type=jnp.float32))
    return jnp.stack(rows_list).astype(jnp.bfloat16)

def reference(cotangent, hidden, context, down_weight, heads_weight, spans):
    masked_values = masked_cotangent(cotangent, spans)
    norm_list = []
    for example in range(EXAMPLE_COUNT):
        norm_list.append(ghost_norm(hidden[example], masked_values[example]) + ghost_norm(context[example], masked_values[example]))
    sq_norm = jnp.stack(norm_list)
    clip_factor = 1.0 / (jnp.sqrt(sq_norm) + GAMMA)
    down_grad = clipped_sum(hidden, masked_values, clip_factor, math.sqrt(FF_W * DW) / EXAMPLE_COUNT)
    heads_grad = clipped_sum(context, masked_values, clip_factor, math.sqrt(HD * DW) / EXAMPLE_COUNT)
    hidden_grad = input_grad(masked_values, down_weight)
    context_grad = input_grad(masked_values, heads_weight)
    return (down_grad, heads_grad, hidden_grad, context_grad)
```

```python
import functools
import math

import jax
import jax.numpy as jnp
from jax import lax
from jax.experimental import pallas as pl
from jax.experimental.pallas import tpu as pltpu
from jax.sharding import PartitionSpec as P

GAMMA = 0.01
VMEM = pltpu.VMEM
F32 = jnp.float32
BF16 = jnp.bfloat16
I16 = jnp.int16
LANES = 128
LIMIT = 48 * 1024 * 1024


def params(grid_dims):
    return pltpu.CompilerParams(
        dimension_semantics=("arbitrary",) * grid_dims, vmem_limit_bytes=LIMIT
    )


def cost(flops, bytes_accessed):
    return pl.CostEstimate(flops=int(flops), bytes_accessed=int(bytes_accessed), transcendentals=0)


def full(shape):
    return pl.BlockSpec(shape, lambda *_: (0,) * len(shape))


def encode_tile(value):
    largest = jnp.max(jnp.abs(value), axis=1, keepdims=True)
    exponent = jnp.ceil(jnp.log2(jnp.maximum(largest, 1e-37))) - 15.0
    exponent = jnp.clip(exponent, -125.0, 120.0)
    scaled = jnp.floor(value * jnp.exp2(-exponent) + 0.5)
    codes = jnp.clip(scaled, -32767.0, 32767.0).astype(jnp.int32).astype(I16)
    return codes, exponent.astype(jnp.int32)


def decode_tile(codes, exponents, index):
    scale = jnp.exp2(exponents[:, index : index + 1].astype(jnp.int32).astype(F32))
    return codes.astype(jnp.int32).astype(F32) * scale


def lane_put(held, index, column):
    lane = lax.broadcasted_iota(jnp.int32, held.shape, 1)
    return jnp.where(lane == index, column, held)


def arrange_kernel(row_count, col_count, spans, *refs):
    pieces, out = refs[:-1], refs[-1]
    r, c = lax.axis_index("row"), lax.axis_index("col")
    examples, held, _ = pieces[0].shape
    per_block = row_count // col_count
    for j, piece in enumerate(pieces):
        source = r ^ j
        block = source // per_block
        k = lax.rem(c - block + col_count, col_count)
        start = pl.multiple_of(lax.rem(source, per_block) * held, held)
        position = source * held + lax.broadcasted_iota(jnp.int32, (held, 1), 0)
        for b in range(examples):
            keep = (position >= spans[b, 0]) & (position < spans[b, 1])
            value = piece[b].astype(F32) * keep.astype(F32)
            out[k, b, pl.ds(start, held), :] = value.astype(BF16)


def arrange(pieces, spans, row_count, col_count):
    examples, held, width = pieces[0].shape
    local = held * row_count // col_count
    shape = (col_count, examples, local, width)
    return pl.pallas_call(
        functools.partial(arrange_kernel, row_count, col_count),
        out_shape=jax.ShapeDtypeStruct(shape, BF16),
        in_specs=[pl.BlockSpec(memory_space=pltpu.SMEM)]
        + [pl.BlockSpec(memory_space=VMEM)] * len(pieces),
        out_specs=pl.BlockSpec(memory_space=VMEM),
        compiler_params=pltpu.CompilerParams(vmem_limit_bytes=LIMIT),
        cost_estimate=cost(0, 4 * math.prod(shape)),
        name="arrange",
    )(spans, *pieces)


def gather_rows(x, row_count):
    near = [x]
    for j in range(2, row_count, 2):
        near.append(lax.ppermute(x, "row", [(i, i ^ j) for i in range(row_count)]))
    pieces = []
    for piece in near:
        pieces.append(piece)
        pieces.append(lax.ppermute(piece, "row", [(i, i ^ 1) for i in range(row_count)]))
    return pieces


def tile_of(*widths):
    return 256 if all(w % 256 == 0 for w in widths) else 128


def partial_kernel(first, last, tile, coded, m_ref, wa_ref, wb_ref, *outs):
    i = pl.program_id(0)
    sums = outs[0]
    ks, rows = sums.shape[0], sums.shape[1]
    masked = m_ref[...].reshape(ks * rows, m_ref.shape[-1])

    def work(w_ref):
        value = lax.dot_general(
            masked, w_ref[...], (((1,), (1,)), ((), ())), preferred_element_type=F32
        )
        for n in range(ks):
            part = value[n * rows : (n + 1) * rows]
            sums[n] = part
            if coded:
                message = outs[1 + n]
                codes, exponent = encode_tile(part)
                message[:, pl.ds(pl.multiple_of(i * tile, tile), tile)] = codes
                side = slice(last * tile, last * tile + LANES)
                held = message[:, side].astype(jnp.int32)
                message[:, side] = lane_put(held, i, exponent).astype(I16)

    @pl.when(i < first)
    def _():
        work(wa_ref)

    @pl.when(i >= first)
    def _():
        work(wb_ref)


def partials(masked, wa, wb, coded):
    ks, examples, local, width = masked.shape
    rows = examples * local
    tile = tile_of(wa.shape[0], wb.shape[0])
    first, last = wa.shape[0] // tile, (wa.shape[0] + wb.shape[0]) // tile
    features = last * tile
    out_shape = [jax.ShapeDtypeStruct((ks, rows, features), F32)]
    out_specs = [pl.BlockSpec((ks, rows, tile), lambda i: (0, 0, i))]
    if coded:
        out_shape += [jax.ShapeDtypeStruct((rows, features + LANES), I16)] * ks
        out_specs += [full((rows, features + LANES))] * ks
    return pl.pallas_call(
        functools.partial(partial_kernel, first, last, tile, coded),
        grid=(last,),
        out_shape=out_shape,
        in_specs=[
            full(masked.shape),
            pl.BlockSpec((tile, width), lambda i: (jnp.minimum(i, first - 1), 0)),
            pl.BlockSpec((tile, width), lambda i: (jnp.maximum(i - first, 0), 0)),
        ],
        out_specs=out_specs,
        compiler_params=params(1),
        cost_estimate=cost(
            2 * ks * rows * width * features, 2 * features * width + 4 * ks * rows * features
        ),
        name="partials",
    )(masked, wa, wb)


def add_kernel(tiles, tile, sums, message, out):
    side = slice(tiles * tile, tiles * tile + LANES)
    exponents = message[:, side]
    held = jnp.zeros(exponents.shape, jnp.int32)
    for n in range(tiles):
        cut = slice(n * tile, (n + 1) * tile)
        value = sums[0, :, cut] + decode_tile(message[:, cut], exponents, n)
        codes, exponent = encode_tile(value)
        out[:, cut] = codes
        held = lane_put(held, n, exponent)
    out[:, side] = held.astype(I16)


def add_message(sums, k, message, tile):
    rows, features = sums.shape[1:]
    step = rows // 4
    return pl.pallas_call(
        functools.partial(add_kernel, features // tile, tile),
        grid=(4,),
        out_shape=jax.ShapeDtypeStruct(message.shape, I16),
        in_specs=[
            pl.BlockSpec((1, step, features), lambda i: (k, i, 0)),
            pl.BlockSpec((step, features + LANES), lambda i: (i, 0)),
        ],
        out_specs=pl.BlockSpec((step, features + LANES), lambda i: (i, 0)),
        compiler_params=params(1),
        cost_estimate=cost(8 * rows * features, 8 * rows * features),
        name="add",
    )(sums, message)


def finish_kernel(tiles, first, tile, sums, right, left, a_ref, b_ref):
    side = slice(tiles * tile, tiles * tile + LANES)
    right_exponents, left_exponents = right[:, side], left[:, side]
    for n in range(tiles):
        cut = slice(n * tile, (n + 1) * tile)
        value = sums[0, :, cut]
        value += decode_tile(right[:, cut], right_exponents, n)
        value += decode_tile(left[:, cut], left_exponents, n)
        if n < first:
            a_ref[0, :, cut] = value.astype(BF16)
        else:
            b_ref[0, :, (n - first) * tile : (n - first + 1) * tile] = value.astype(BF16)


def finish(sums, k, right, left, examples, widths, tile):
    rows, features = sums.shape[1:]
    local = rows // examples
    half = local // 2
    message = pl.BlockSpec((half, features + LANES), lambda i: (i, 0))
    return pl.pallas_call(
        functools.partial(finish_kernel, features // tile, widths[0] // tile, tile),
        grid=(2 * examples,),
        out_shape=[jax.ShapeDtypeStruct((examples, local, w), BF16) for w in widths],
        in_specs=[pl.BlockSpec((1, half, features), lambda i: (k, i, 0)), message, message],
        out_specs=[pl.BlockSpec((1, half, w), lambda i: (i // 2, i % 2, 0)) for w in widths],
        compiler_params=params(1),
        cost_estimate=cost(8 * rows * features, 10 * rows * features),
        name="finish",
    )(sums, right, left)


def norm_kernel(col_count, *refs):
    m_ref, own = refs[0], refs[1]
    rights, lefts = refs[2 : 1 + col_count], refs[1 + col_count : 2 * col_count]
    out = refs[-1]
    nt = (((1,), (1,)), ((), ()))
    lane = lax.broadcasted_iota(jnp.int32, out.shape, 1)
    total = jnp.zeros(out.shape, F32)
    for b in range(own.shape[0]):
        parts = [own[b]]
        for k in range(1, col_count):
            parts.append(rights[k - 1][b] + lefts[col_count - k - 1][b])
        feature = jnp.concatenate(parts, axis=0)
        masked = m_ref[:, b].reshape(feature.shape[0], m_ref.shape[-1])
        left_gram = lax.dot_general(feature, feature, nt, preferred_element_type=F32)
        right_gram = lax.dot_general(masked, masked, nt, preferred_element_type=F32)
        total = jnp.where(lane == b, jnp.sum(left_gram * right_gram), total)
    out[...] = total


def local_norm(masked, own, rights, lefts):
    col_count = masked.shape[0]
    arrays = [masked, own, *rights, *lefts]
    return pl.pallas_call(
        functools.partial(norm_kernel, col_count),
        out_shape=jax.ShapeDtypeStruct((8, LANES), F32),
        in_specs=[pl.BlockSpec(memory_space=VMEM)] * len(arrays),
        out_specs=pl.BlockSpec(memory_space=VMEM),
        compiler_params=pltpu.CompilerParams(vmem_limit_bytes=LIMIT),
        cost_estimate=cost(2 * 10**9, 8 * 10**6),
        name="norm",
    )(*arrays)


def sum_over(x, axis, count):
    j = 1
    while j < count:
        x = x + lax.ppermute(x, axis, [(i, i ^ j) for i in range(count)])
        j *= 2
    return x


def weight_kernel(col_count, first, scales, factor, *refs):
    m_ref, own = refs[0], refs[1]
    rights, lefts = refs[2 : 1 + col_count], refs[1 + col_count : 2 * col_count]
    a_ref, b_ref = refs[-2:]
    i = pl.program_id(0)
    total = None
    for b in range(own.shape[0]):
        parts = [own[b]]
        for k in range(1, col_count):
            parts.append(rights[k - 1][b] + lefts[col_count - k - 1][b])
        feature = jnp.concatenate(parts, axis=0)
        masked = m_ref[:, b].reshape(feature.shape[0], m_ref.shape[-1])
        each = lax.dot_general(
            feature, masked, (((0,), (0,)), ((), ())), preferred_element_type=F32
        )
        each = factor[0, b] * each
        total = each if total is None else total + each

    @pl.when(i < first)
    def _():
        a_ref[...] = total * scales[0]

    @pl.when(i >= first)
    def _():
        b_ref[...] = total * scales[1]


def weight_grads(factor, masked, own, rights, lefts, widths, scales):
    col_count, examples, local, width = masked.shape
    tile = tile_of(*widths)
    first, last = widths[0] // tile, sum(widths) // tile
    block = pl.BlockSpec((examples, local, tile), lambda i: (0, 0, i))
    count = 2 * col_count - 1
    return pl.pallas_call(
        functools.partial(weight_kernel, col_count, first, scales),
        grid=(last,),
        out_shape=[jax.ShapeDtypeStruct((w, width), F32) for w in widths],
        in_specs=[pl.BlockSpec(memory_space=pltpu.SMEM), full(masked.shape)] + [block] * count,
        out_specs=[
            pl.BlockSpec((tile, width), lambda i: (jnp.minimum(i, first - 1), 0)),
            pl.BlockSpec((tile, width), lambda i: (jnp.maximum(i - first, 0), 0)),
        ],
        compiler_params=params(1),
        cost_estimate=cost(
            2 * examples * local * col_count * width * sum(widths), 4 * width * sum(widths)
        ),
        name="weights",
    )(factor, masked, own, *rights, *lefts)


def body(row_count, col_count, scales, cotangent, hidden, context, wa, wb, spans):
    n = col_count
    widths = (hidden.shape[2], context.shape[2])
    examples = hidden.shape[0]
    tile = tile_of(*widths)
    own = jnp.concatenate([hidden, context], axis=2)

    def send_right(x, low, high):
        return lax.ppermute(x, "col", [(i, i + 1) for i in range(low, high)])

    def send_left(x, low, high):
        return lax.ppermute(x, "col", [(i, i - 1) for i in range(low, high)])

    rights, lefts = [send_right(own, 0, n - 1)], [send_left(own, 1, n)]
    masked = arrange(gather_rows(cotangent, row_count), spans, row_count, n)

    outer = jnp.stack([masked[1], masked[n - 1]])
    outer_sums, right_message, left_message = partials(outer, wa, wb, True)
    inner = [k for k in range(n) if k not in (1, n - 1)]
    inner_sums = partials(jnp.stack([masked[k] for k in inner]), wa, wb, False)[0]

    def sums_of(k):
        if k in (1, n - 1):
            return outer_sums, (0 if k == 1 else 1)
        return inner_sums, inner.index(k)

    right_came = left_came = None
    for s in range(1, n):
        if s > 1:
            sums, at = sums_of(s)
            right_message = add_message(sums, at, right_came, tile)
            sums, at = sums_of(n - s)
            left_message = add_message(sums, at, left_came, tile)
        if s < n - 1:
            rights.append(send_right(rights[-1], s, n - 1))
            lefts.append(send_left(lefts[-1], 1, n - s))
        right_came = send_right(right_message, 0, s)
        left_came = send_left(left_message, n - s, n)

    sq_norm = local_norm(masked, own, rights, lefts)
    sq_norm = sum_over(sum_over(sq_norm, "row", row_count), "col", n)
    factor = 1.0 / (jnp.sqrt(sq_norm[:1, :examples]) + GAMMA)
    down_grad, heads_grad = weight_grads(factor, masked, own, rights, lefts, widths, scales)
    sums, at = sums_of(0)
    hidden_grad, context_grad = finish(sums, at, right_came, left_came, examples, widths, tile)
    return down_grad, heads_grad, hidden_grad, context_grad


def solution(mesh):
    row_count, col_count = mesh.shape["row"], mesh.shape["col"]

    def run(cotangent, hidden, context, down_weight, heads_weight, spans):
        examples = hidden.shape[0]
        scales = tuple(math.sqrt(w.shape[0] * w.shape[1]) / examples for w in (down_weight, heads_weight))
        in_specs = (
            P(None, "row", "col"),
            P(None, "col", "row"),
            P(None, "col", "row"),
            P("row", "col"),
            P("row", "col"),
            P(),
        )
        out_specs = (P("row", "col"), P("row", "col"), P(None, "col", "row"), P(None, "col", "row"))
        return jax.shard_map(
            functools.partial(body, row_count, col_count, scales),
            mesh=mesh,
            in_specs=in_specs,
            out_specs=out_specs,
            check_vma=False,
        )(cotangent, hidden, context, down_weight, heads_weight, spans)

    return run
```

```python
import functools
import math

import jax
import jax.numpy as jnp
from jax import lax
from jax.experimental import pallas as pl
from jax.experimental.pallas import tpu as pltpu
from jax.sharding import PartitionSpec as P

GAMMA = 0.01
VMEM = pltpu.VMEM
F32 = jnp.float32
BF16 = jnp.bfloat16
I16 = jnp.int16
LANES = 128
LIMIT = 32 * 1024 * 1024


def params(grid_dims):
    return pltpu.CompilerParams(
        dimension_semantics=("arbitrary",) * grid_dims, vmem_limit_bytes=LIMIT
    )


def cost(bytes_accessed):
    return pl.CostEstimate(flops=int(300 * bytes_accessed), bytes_accessed=int(bytes_accessed), transcendentals=0)


def held_back(kernel, count):
    def run(*refs, operands):
        kernel(*refs[: operands - count], *refs[operands:])

    return run


def call(kernel, arrays, specs, deps=(), **rest):
    operands = len(arrays) + len(deps)
    if deps:
        kernel = functools.partial(held_back(kernel, len(deps)), operands=operands)
    specs = list(specs) + [pl.BlockSpec(memory_space=pl.ANY)] * len(deps)
    return pl.pallas_call(kernel, in_specs=specs, **rest)(*arrays, *deps)


def full(shape):
    return pl.BlockSpec(shape, lambda *_: (0,) * len(shape))


class Chunk:
    def __init__(self, parts):
        self.parts = parts
        self.width = sum(p[2] for p in parts)
        self.groups = []
        column = 0
        for _, _, size in parts:
            count = -(-size // 1024)
            tiles = size // LANES
            for g in range(count):
                begin, end = tiles * g // count, tiles * (g + 1) // count
                self.groups.append((column + begin * LANES, (end - begin) * LANES))
            column += size
        self.message = self.width + LANES

    def places(self):
        column = 0
        for which, first, size in self.parts:
            for at in range(0, size, LANES):
                yield column + at, which, first + at
            column += size


TOP = 32760.0


def encode(chunk, value, out, start, rows):
    lane = lax.broadcasted_iota(jnp.int32, (rows, LANES), 1)
    side = jnp.zeros((rows, LANES), F32)
    at = pl.ds(start, rows)
    for g, (first, size) in enumerate(chunk.groups):
        values = [value(column) for column in range(first, first + size, LANES)]
        largest = jnp.abs(values[0])
        for v in values[1:]:
            largest = jnp.maximum(largest, jnp.abs(v))
        largest = jnp.max(largest, axis=1, keepdims=True)
        exponent = jnp.clip(jnp.ceil(jnp.log2(jnp.maximum(largest, 1e-37))), -110.0, 126.0)
        mantissa = jnp.floor(largest * jnp.exp2(-exponent) * 8192.0) + 2.0
        inverse = jnp.broadcast_to((TOP * 8192.0 / mantissa) * jnp.exp2(-exponent), (rows, LANES))
        side = jnp.where(lane == 2 * g, exponent, jnp.where(lane == 2 * g + 1, mantissa, side))
        for n, v in enumerate(values):
            codes = jnp.floor(v * inverse + 0.5).astype(jnp.int32).astype(I16)
            out[at, first + n * LANES : first + (n + 1) * LANES] = codes
    out[at, chunk.width :] = side.astype(jnp.int32).astype(I16)


def decoder(chunk, message, start, rows):
    at = pl.ds(start, rows)
    side = message[at, chunk.width :].astype(jnp.int32).astype(F32)
    scales = []
    for g in range(len(chunk.groups)):
        scale = jnp.exp2(side[:, 2 * g : 2 * g + 1]) * (side[:, 2 * g + 1 : 2 * g + 2] / (TOP * 8192.0))
        scales.append(jnp.broadcast_to(scale, (rows, LANES)))

    def value(column):
        g = [i for i, (first, size) in enumerate(chunk.groups) if first <= column < first + size][0]
        return message[at, column : column + LANES].astype(jnp.int32).astype(F32) * scales[g]

    return value


def code_kernel(chunk, step, hidden, context, out):
    arrays = (hidden, context)
    places = {column: (which, at) for column, which, at in chunk.places()}
    local = hidden.shape[1]
    for b in range(hidden.shape[0]):
        for start in range(0, local, step):

            def value(column):
                which, at = places[column]
                return arrays[which][b, start : start + step, at : at + LANES].astype(F32)

            encode(chunk, value, out, b * local + start, step)


def code_own(chunk, hidden, context, deps=()):
    examples, local, _ = hidden.shape
    rows = examples * local
    return call(
        functools.partial(code_kernel, chunk, 16),
        (hidden, context),
        [pl.BlockSpec(memory_space=VMEM)] * 2,
        deps,
        out_shape=jax.ShapeDtypeStruct((rows, chunk.message), I16),
        out_specs=pl.BlockSpec(memory_space=VMEM),
        compiler_params=pltpu.CompilerParams(vmem_limit_bytes=16 * 2**20),
        cost_estimate=cost(4e6),
        name="code",
    )


def place(n):
    c = lax.axis_index("col")
    return jnp.where(lax.axis_index("row") % 2 == 0, c, n - 1 - c)


def flow_pairs(n, row_count, flow):
    pairs = []
    for row in range(row_count):
        for c in range(n - 1):
            low, high = row * n + c, row * n + c + 1
            pairs.append((low, high) if (row % 2 == 0) == (flow == 0) else (high, low))
    return pairs


def arrange_kernel(row_count, col_count, spans, *refs):
    pieces, out = refs[:-1], refs[-1]
    r, c = lax.axis_index("row"), lax.axis_index("col")
    examples, held, _ = pieces[0].shape
    per_block = row_count // col_count
    for j, piece in enumerate(pieces):
        source = r ^ j
        block = source // per_block
        k = jnp.where(r % 2 == 0, c - block, block - c)
        k = lax.rem(k + col_count, col_count)
        start = pl.multiple_of(lax.rem(source, per_block) * held, held)
        position = source * held + lax.broadcasted_iota(jnp.int32, (held, 1), 0)
        for b in range(examples):
            keep = (position >= spans[b, 0]) & (position < spans[b, 1])
            value = piece[b].astype(F32) * keep.astype(F32)
            out[k, b, pl.ds(start, held), :] = value.astype(BF16)


def arrange(pieces, spans, row_count, col_count):
    examples, held, width = pieces[0].shape
    local = held * row_count // col_count
    shape = (col_count, examples, local, width)
    return pl.pallas_call(
        functools.partial(arrange_kernel, row_count, col_count),
        out_shape=jax.ShapeDtypeStruct(shape, BF16),
        in_specs=[pl.BlockSpec(memory_space=pltpu.SMEM)]
        + [pl.BlockSpec(memory_space=VMEM)] * len(pieces),
        out_specs=pl.BlockSpec(memory_space=VMEM),
        compiler_params=pltpu.CompilerParams(vmem_limit_bytes=LIMIT),
        cost_estimate=cost(4e6),
        name="arrange",
    )(spans, *pieces)


def after(x, *others):
    return lax.optimization_barrier((x, *others))[0]


def after(x, *others):
    return lax.optimization_barrier((x, *others))[0]


def gather_rows(x, row_count, others):
    near = [x]
    for j in range(2, row_count, 2):
        near.append(lax.ppermute(x, "row", [(i, i ^ j) for i in range(row_count)]))
    pieces = []
    for j, piece in enumerate(near):
        if j > 0:
            piece = after(piece, *others)
        pieces.append(piece)
        pieces.append(lax.ppermute(piece, "row", [(i, i ^ 1) for i in range(row_count)]))
    return pieces


def pieces_of(size):
    cut = (size // LANES + 1) // 2 * LANES if size > 1024 else size
    return [(0, cut)] + ([(cut, size - cut)] if cut < size else [])


def partial_kernel(plan, ks, m_ref, wa, wb, out, held, sems):
    weights = (wa, wb)
    copies = []
    for number, (which, source, start, size) in enumerate(plan):
        copy = pltpu.make_async_copy(
            weights[which].at[pl.ds(source, size)], held.at[pl.ds(start, size)], sems.at[number]
        )
        copy.start()
        copies.append(copy)
    rows = out.shape[1]
    p = place(m_ref.shape[0])
    masked = jnp.concatenate(
        [m_ref[pl.ds(k(p), 1)].reshape(rows, m_ref.shape[-1]) for k in ks], axis=0
    )
    for copy, (_, _, start, size) in zip(copies, plan):
        copy.wait()
        value = lax.dot_general(
            masked, held[pl.ds(start, size)], NT, preferred_element_type=F32
        )
        for n in range(len(ks)):
            out[n, :, start : start + size] = value[n * rows : (n + 1) * rows]


def partials(chunk, masked, ks, wa, wb, bytes_accessed, deps=()):
    _, examples, local, width = masked.shape
    rows = examples * local
    plan, column = [], 0
    for which, first, count in chunk.parts:
        for start, size in pieces_of(count):
            plan.append((which, first + start, column + start, size))
        column += count
    return call(
        functools.partial(partial_kernel, plan, ks),
        (masked, wa, wb),
        [pl.BlockSpec(memory_space=VMEM)] + [pl.BlockSpec(memory_space=pl.ANY)] * 2,
        deps,
        out_shape=jax.ShapeDtypeStruct((len(ks), rows, chunk.width), F32),
        out_specs=pl.BlockSpec(memory_space=VMEM),
        scratch_shapes=[
            pltpu.VMEM((chunk.width, width), BF16),
            pltpu.SemaphoreType.DMA((len(plan),)),
        ],
        compiler_params=pltpu.CompilerParams(vmem_limit_bytes=40 * 2**20),
        cost_estimate=cost(bytes_accessed),
        name="partials",
    )


STEPS = 2
FIRST = 4e6
ROWS = 16


def outer_made_first(n, k):
    early = place(n) < n // 2
    return early if k == 1 else jnp.logical_not(early)


def next_kernel(chunk, n, s, flow, keys, *refs):
    sums, (came, out) = dict(zip(keys, refs)), refs[len(keys) :]
    k = s if flow == 0 else n - s
    mine = place(n) if flow == 0 else n - 1 - place(n)
    rows = came.shape[0]

    @pl.when((mine >= s) & (mine < n - 1))
    def _():
        out[...] = came[...]

    def add(held):
        def one(i, carry):
            start = pl.multiple_of(i * ROWS, ROWS)
            old = decoder(chunk, came, start, ROWS)

            def value(column):
                return held[0, pl.ds(start, ROWS), column : column + LANES] + old(column)

            encode(chunk, value, out, start, ROWS)
            return carry

        lax.fori_loop(0, rows // ROWS, one, 0)

    if ("second", 0) not in sums:

        @pl.when(mine < s)
        def _():
            add(sums[keys[0]])

    else:

        @pl.when((mine < s) & outer_made_first(n, k))
        def _():
            add(sums["first", 0])

        @pl.when((mine < s) & jnp.logical_not(outer_made_first(n, k)))
        def _():
            add(sums["second", 0])


def next_message(chunk, n, s, flow, first, second, came, deps=()):
    rows = came.shape[0]
    step = rows // STEPS
    k = s if flow == 0 else n - s
    keys = [("first", 0 if k in (1, n - 1) else k - 1)]
    if s == n - 1 and s > 1:
        keys.append(("second", 0))
    message = pl.BlockSpec((step, chunk.message), lambda i: (i, 0))
    return call(
        functools.partial(next_kernel, chunk, n, s, flow, keys),
        [first if which == "first" else second for which, _ in keys] + [came],
        [pl.BlockSpec((1, step, chunk.width), lambda i, at=at: (at, i, 0)) for _, at in keys]
        + [message],
        deps,
        grid=(STEPS,),
        out_shape=jax.ShapeDtypeStruct(came.shape, I16),
        out_specs=message,
        compiler_params=params(1),
        cost_estimate=cost(40e6),
        name="next",
    )


def finish_kernel(chunks, at, *refs):
    count = len(chunks)
    sums, rights, lefts = refs[:count], refs[count : 2 * count], refs[2 * count : 3 * count]
    outs = refs[3 * count :]
    rows = rights[0].shape[0]
    for start in range(0, rows, ROWS):
        for chunk, total, right, left in zip(chunks, sums, rights, lefts):
            old_right = decoder(chunk, right, start, ROWS)
            old_left = decoder(chunk, left, start, ROWS)
            for column, which, place in chunk.places():
                value = total[0, start : start + ROWS, column : column + LANES]
                value = value + old_right(column) + old_left(column)
                outs[which][0, start : start + ROWS, place : place + LANES] = value.astype(BF16)


def finish(chunks, sums, at, rights, lefts, examples, widths, deps=()):
    rows = sums[0].shape[1]
    local = rows // examples
    half = local // 2
    return call(
        functools.partial(finish_kernel, chunks, at),
        [*sums, *rights, *lefts],
        [pl.BlockSpec((1, half, x.shape[2]), lambda i: (at, i, 0)) for x in sums]
        + [pl.BlockSpec((half, x.shape[1]), lambda i: (i, 0)) for x in (*rights, *lefts)],
        deps,
        grid=(2 * examples,),
        out_shape=[jax.ShapeDtypeStruct((examples, local, w), BF16) for w in widths],
        out_specs=[pl.BlockSpec((1, half, w), lambda i: (i // 2, i % 2, 0)) for w in widths],
        compiler_params=params(1),
        cost_estimate=cost(8e6),
        name="finish",
    )


NT = (((1,), (1,)), ((), ()))


def gram_kernel(m_ref, out):
    for b in range(out.shape[0]):
        masked = m_ref[:, b].reshape(out.shape[1], m_ref.shape[-1])
        out[b] = lax.dot_general(masked, masked, NT, preferred_element_type=F32)


def gram(masked, deps=()):
    col_count, examples, local, width = masked.shape
    length = col_count * local
    return call(
        gram_kernel,
        (masked,),
        [pl.BlockSpec(memory_space=VMEM)],
        deps,
        out_shape=jax.ShapeDtypeStruct((examples, length, length), F32),
        out_specs=pl.BlockSpec(memory_space=VMEM),
        compiler_params=pltpu.CompilerParams(vmem_limit_bytes=16 * 2**20),
        cost_estimate=cost(3e6),
        name="gram",
    )


def join_kernel(chunk, n, gram_ref, hidden, context, *refs):
    rights, lefts = refs[: n - 1], refs[n - 1 : 2 * n - 2]
    joined, out = refs[-2:]
    p = place(n)
    arrays = (hidden, context)
    examples, local, _ = hidden.shape
    for column, which, at in chunk.places():
        joined[:, :local, column : column + LANES] = arrays[which][:, :, at : at + LANES]

    def take(k, message):
        for b in range(examples):

            def one(i, carry):
                start = pl.multiple_of(i * ROWS, ROWS)
                value = decoder(chunk, message, b * local + start, ROWS)
                for column in range(0, chunk.width, LANES):
                    joined[b, pl.ds(k * local + start, ROWS), column : column + LANES] = value(
                        column
                    ).astype(BF16)
                return carry

            lax.fori_loop(0, local // ROWS, one, 0)

    for k in range(1, n):

        @pl.when(p >= k)
        def _():
            take(k, rights[k - 1])

        @pl.when(p < k)
        def _():
            take(k, lefts[n - k - 1])

    lane = lax.broadcasted_iota(jnp.int32, out.shape, 1)
    total = jnp.zeros(out.shape, F32)
    for b in range(examples):
        feature = joined[b]
        feature_gram = lax.dot_general(feature, feature, NT, preferred_element_type=F32)
        total = jnp.where(lane == b, jnp.sum(feature_gram * gram_ref[b]), total)
    out[...] = total


def join(chunk, masked_gram, hidden, context, rights, lefts, deps=()):
    n = len(rights) + 1
    examples, local, _ = hidden.shape
    arrays = [masked_gram, hidden, context, *rights, *lefts]
    shape = (examples, n * local, chunk.width)
    return call(
        functools.partial(join_kernel, chunk, n),
        arrays,
        [pl.BlockSpec(memory_space=VMEM)] * len(arrays),
        deps,
        out_shape=[jax.ShapeDtypeStruct(shape, BF16), jax.ShapeDtypeStruct((8, LANES), F32)],
        out_specs=[pl.BlockSpec(memory_space=VMEM)] * 2,
        compiler_params=pltpu.CompilerParams(vmem_limit_bytes=24 * 2**20),
        cost_estimate=cost(16e6),
        name="join",
    )


def sum_over(x, axis, count, groups):
    for group in groups:
        came = [lax.ppermute(x, axis, [(i, i ^ j) for i in range(count)]) for j in group]
        came = lax.optimization_barrier(came)
        for y in came:
            x = x + y
    return x


def weight_kernel(widths, factor, m_ref, *refs):
    features, outs = refs[:-2], refs[-2:]
    examples, length = features[0].shape[:2]
    masked = [m_ref[:, b].reshape(length, m_ref.shape[-1]) for b in range(examples)]
    column = 0
    for x in features:
        for start in range(0, x.shape[2], LANES):
            out, at = (0, column) if column < widths[0] else (1, column - widths[0])
            total = None
            for b in range(examples):
                each = lax.dot_general(
                    x[b, :, start : start + LANES],
                    masked[b],
                    (((0,), (0,)), ((), ())),
                    preferred_element_type=F32,
                )
                each = factor[out, b] * each
                total = each if total is None else total + each
            outs[out][at : at + LANES] = total
            column += LANES


def weight_grads(factor, masked, features, widths):
    col_count, examples, local, width = masked.shape
    tile = min(256, width)
    whole = lambda x: pl.BlockSpec(x.shape, lambda i: (0, 0, 0), pipeline_mode=pl.Buffered(1))
    return pl.pallas_call(
        functools.partial(weight_kernel, widths),
        grid=(width // tile,),
        out_shape=[jax.ShapeDtypeStruct((w, width), F32) for w in widths],
        in_specs=[
            pl.BlockSpec(memory_space=pltpu.SMEM),
            pl.BlockSpec((col_count, examples, local, tile), lambda i: (0, 0, 0, i)),
        ]
        + [whole(x) for x in features],
        out_specs=[pl.BlockSpec((w, tile), lambda i: (0, i)) for w in widths],
        compiler_params=params(1),
        cost_estimate=cost(48e6),
        name="weights",
    )(factor, masked, *features)


def body(row_count, col_count, scales, cotangent, hidden, context, wa, wb, spans):
    n = col_count
    widths = (hidden.shape[2], context.shape[2])
    examples = hidden.shape[0]
    chunk = Chunk([(0, 0, widths[0]), (1, 0, widths[1])])

    def send(x, flow):
        return lax.ppermute(x, ("row", "col"), flow_pairs(n, row_count, flow))

    own = code_own(chunk, hidden, context)
    came = [[send(own, 0)], [send(own, 1)]]
    masked = arrange(gather_rows(cotangent, row_count, (own,)), spans, row_count, n)

    first_ks = [lambda p: jnp.where(p < n // 2, 1, n - 1)]
    first_ks += [lambda p, k=k: k for k in range(2, n - 1)]
    second_ks = [lambda p: jnp.where(p < n // 2, n - 1, 1), lambda p: 0]
    first = partials(chunk, masked, first_ks, wa, wb, FIRST)
    second, latest = None, ()
    for s in range(1, n):
        if s == n - 1:
            second = partials(chunk, masked, second_ks, wa, wb, 4e6, latest)
            masked_gram = gram(masked, (second,))
            latest = (second,)
        for flow in (0, 1):
            message = next_message(chunk, n, s, flow, first, second, came[flow][-1], latest)
            latest = (message,)
            came[flow].append(send(message, flow))

    joined = [
        join(chunk, masked_gram, hidden, context, came[0][:-1], came[1][:-1], latest)
    ]
    sq_norm = sum(j[1] for j in joined)
    sq_norm = sum_over(sq_norm, "row", row_count, [[1], range(2, row_count, 2)])
    sq_norm = after(sq_norm, came[0][-1])
    sq_norm = sum_over(sq_norm, "col", n, [range(1, n)])
    factor = 1.0 / (jnp.sqrt(sq_norm[0, :examples]) + GAMMA)
    factor = jnp.stack([factor * scale for scale in scales])
    down_grad, heads_grad = weight_grads(factor, masked, [j[0] for j in joined], widths)
    hidden_grad, context_grad = finish(
        [chunk], [second], 1, [came[0][-1]], [came[1][-1]], examples, widths, (factor,)
    )
    return down_grad, heads_grad, hidden_grad, context_grad


def solution(mesh):
    row_count, col_count = mesh.shape["row"], mesh.shape["col"]

    def run(cotangent, hidden, context, down_weight, heads_weight, spans):
        examples = hidden.shape[0]
        scales = tuple(math.sqrt(w.shape[0] * w.shape[1]) / examples for w in (down_weight, heads_weight))
        in_specs = (
            P(None, "row", "col"),
            P(None, "col", "row"),
            P(None, "col", "row"),
            P("row", "col"),
            P("row", "col"),
            P(),
        )
        out_specs = (P("row", "col"), P("row", "col"), P(None, "col", "row"), P(None, "col", "row"))
        return jax.shard_map(
            functools.partial(body, row_count, col_count, scales),
            mesh=mesh,
            in_specs=in_specs,
            out_specs=out_specs,
            check_vma=False,
        )(cotangent, hidden, context, down_weight, heads_weight, spans)

    return run
```

```python
import functools
import math

import jax
import jax.numpy as jnp
from jax import lax
from jax.experimental import pallas as pl
from jax.experimental.pallas import tpu as pltpu
from jax.sharding import PartitionSpec as P

GAMMA = 0.01
VMEM = pltpu.VMEM
F32 = jnp.float32
BF16 = jnp.bfloat16
I16 = jnp.int16
LANES = 128


def params(grid_dims, mebibytes):
    return pltpu.CompilerParams(
        dimension_semantics=("arbitrary",) * grid_dims, vmem_limit_bytes=mebibytes * 2**20
    )


def cost(bytes_accessed):
    return pl.CostEstimate(flops=int(300 * bytes_accessed), bytes_accessed=int(bytes_accessed), transcendentals=0)


def held_back(kernel, count):
    def run(*refs, operands):
        kernel(*refs[: operands - count], *refs[operands:])

    return run


def call(kernel, arrays, specs, deps=(), **rest):
    operands = len(arrays) + len(deps)
    if deps:
        kernel = functools.partial(held_back(kernel, len(deps)), operands=operands)
    specs = list(specs) + [pl.BlockSpec(memory_space=pl.ANY)] * len(deps)
    return pl.pallas_call(kernel, in_specs=specs, **rest)(*arrays, *deps)


def full(shape):
    return pl.BlockSpec(shape, lambda *_: (0,) * len(shape))


class Chunk:
    def __init__(self, parts):
        self.parts = parts
        self.width = sum(p[2] for p in parts)
        self.groups = []
        column = 0
        for _, _, size in parts:
            count = -(-size // 1024)
            tiles = size // LANES
            for g in range(count):
                begin, end = tiles * g // count, tiles * (g + 1) // count
                self.groups.append((column + begin * LANES, (end - begin) * LANES))
            column += size
        self.message = self.width + LANES

    def places(self):
        column = 0
        for which, first, size in self.parts:
            for at in range(0, size, LANES):
                yield column + at, which, first + at
            column += size


TOP = 32760.0


def encode(chunk, value, out, start, rows):
    lane = lax.broadcasted_iota(jnp.int32, (rows, LANES), 1)
    side = jnp.zeros((rows, LANES), F32)
    at = pl.ds(start, rows)
    for g, (first, size) in enumerate(chunk.groups):
        values = [value(column) for column in range(first, first + size, LANES)]
        largest = jnp.abs(values[0])
        for v in values[1:]:
            largest = jnp.maximum(largest, jnp.abs(v))
        largest = jnp.max(largest, axis=1, keepdims=True)
        exponent = jnp.clip(jnp.ceil(jnp.log2(jnp.maximum(largest, 1e-37))), -110.0, 126.0)
        mantissa = jnp.floor(largest * jnp.exp2(-exponent) * 8192.0) + 2.0
        inverse = jnp.broadcast_to((TOP * 8192.0 / mantissa) * jnp.exp2(-exponent), (rows, LANES))
        side = jnp.where(lane == 2 * g, exponent, jnp.where(lane == 2 * g + 1, mantissa, side))
        for n, v in enumerate(values):
            codes = jnp.floor(v * inverse + 0.5).astype(jnp.int32).astype(I16)
            out[at, first + n * LANES : first + (n + 1) * LANES] = codes
    out[at, chunk.width :] = side.astype(jnp.int32).astype(I16)


def decoder(chunk, message, start, rows):
    at = pl.ds(start, rows)
    side = message[at, chunk.width :].astype(jnp.int32).astype(F32)
    scales = []
    for g in range(len(chunk.groups)):
        scale = jnp.exp2(side[:, 2 * g : 2 * g + 1]) * (side[:, 2 * g + 1 : 2 * g + 2] / (TOP * 8192.0))
        scales.append(jnp.broadcast_to(scale, (rows, LANES)))

    def value(column):
        g = [i for i, (first, size) in enumerate(chunk.groups) if first <= column < first + size][0]
        return message[at, column : column + LANES].astype(jnp.int32).astype(F32) * scales[g]

    return value


def code_kernel(chunk, step, hidden, context, out):
    arrays = (hidden, context)
    places = {column: (which, at) for column, which, at in chunk.places()}
    local = hidden.shape[1]
    for b in range(hidden.shape[0]):
        for start in range(0, local, step):

            def value(column):
                which, at = places[column]
                return arrays[which][b, start : start + step, at : at + LANES].astype(F32)

            encode(chunk, value, out, b * local + start, step)


def code_own(chunk, hidden, context, deps=()):
    examples, local, _ = hidden.shape
    rows = examples * local
    return call(
        functools.partial(code_kernel, chunk, 16),
        (hidden, context),
        [pl.BlockSpec(memory_space=VMEM)] * 2,
        deps,
        out_shape=jax.ShapeDtypeStruct((rows, chunk.message), I16),
        out_specs=pl.BlockSpec(memory_space=VMEM),
        compiler_params=pltpu.CompilerParams(vmem_limit_bytes=16 * 2**20),
        cost_estimate=cost(20e6),
        name="code",
    )


def place(n):
    c = lax.axis_index("col")
    return jnp.where(lax.axis_index("row") % 2 == 0, c, n - 1 - c)


def flow_pairs(n, row_count, flow):
    pairs = []
    for row in range(row_count):
        for c in range(n - 1):
            low, high = row * n + c, row * n + c + 1
            pairs.append((low, high) if (row % 2 == 0) == (flow == 0) else (high, low))
    return pairs


def arrange_kernel(row_count, col_count, spans, *refs):
    pieces, out = refs[:-1], refs[-1]
    r, c = lax.axis_index("row"), lax.axis_index("col")
    examples, held, _ = pieces[0].shape
    per_block = row_count // col_count
    for j, piece in enumerate(pieces):
        source = r ^ j
        block = source // per_block
        k = jnp.where(r % 2 == 0, c - block, block - c)
        k = lax.rem(k + col_count, col_count)
        start = pl.multiple_of(lax.rem(source, per_block) * held, held)
        position = source * held + lax.broadcasted_iota(jnp.int32, (held, 1), 0)
        for b in range(examples):
            keep = (position >= spans[b, 0]) & (position < spans[b, 1])
            value = piece[b].astype(F32) * keep.astype(F32)
            out[k, b, pl.ds(start, held), :] = value.astype(BF16)


def arrange(pieces, spans, row_count, col_count):
    examples, held, width = pieces[0].shape
    local = held * row_count // col_count
    shape = (col_count, examples, local, width)
    return pl.pallas_call(
        functools.partial(arrange_kernel, row_count, col_count),
        out_shape=jax.ShapeDtypeStruct(shape, BF16),
        in_specs=[pl.BlockSpec(memory_space=pltpu.SMEM)]
        + [pl.BlockSpec(memory_space=VMEM)] * len(pieces),
        out_specs=pl.BlockSpec(memory_space=VMEM),
        compiler_params=pltpu.CompilerParams(vmem_limit_bytes=12 * 2**20),
        cost_estimate=cost(20e6),
        name="arrange",
    )(spans, *pieces)


def after(x, *others):
    return lax.optimization_barrier((x, *others))[0]


def after(x, *others):
    return lax.optimization_barrier((x, *others))[0]


def gather_rows(x, row_count, others):
    near = [x]
    for j in range(2, row_count, 2):
        near.append(lax.ppermute(x, "row", [(i, i ^ j) for i in range(row_count)]))
    pieces = []
    for j, piece in enumerate(near):
        if j > 0:
            piece = after(piece, *others)
        pieces.append(piece)
        pieces.append(lax.ppermute(piece, "row", [(i, i ^ 1) for i in range(row_count)]))
    return pieces


PIECE = 512
RING = 4


def pieces_of(size):
    return [(start, min(PIECE, size - start)) for start in range(0, size, PIECE)]


def partial_kernel(plan, ks, m_ref, wa, wb, out, held, sems):
    weights = (wa, wb)

    def copy(number):
        which, source, _, size = plan[number]
        slot = number % RING
        return pltpu.make_async_copy(
            weights[which].at[pl.ds(source, size)], held.at[slot, pl.ds(0, size)], sems.at[slot]
        )

    for number in range(min(RING, len(plan))):
        copy(number).start()
    rows = out.shape[1]
    p = place(m_ref.shape[0])
    masked = jnp.concatenate(
        [m_ref[pl.ds(k(p), 1)].reshape(rows, m_ref.shape[-1]) for k in ks], axis=0
    )
    for number, (_, _, start, size) in enumerate(plan):
        copy(number).wait()
        value = lax.dot_general(
            masked, held[number % RING, pl.ds(0, size)], NT, preferred_element_type=F32
        )
        for n in range(len(ks)):
            out[n, :, start : start + size] = value[n * rows : (n + 1) * rows]
        if number + RING < len(plan):
            copy(number + RING).start()


def partials(chunk, masked, ks, wa, wb, bytes_accessed, deps=()):
    _, examples, local, width = masked.shape
    rows = examples * local
    plan, column = [], 0
    for which, first, count in chunk.parts:
        for start, size in pieces_of(count):
            plan.append((which, first + start, column + start, size))
        column += count
    return call(
        functools.partial(partial_kernel, plan, ks),
        (masked, wa, wb),
        [pl.BlockSpec(memory_space=VMEM)] + [pl.BlockSpec(memory_space=pltpu.HBM)] * 2,
        deps,
        out_shape=jax.ShapeDtypeStruct((len(ks), rows, chunk.width), F32),
        out_specs=pl.BlockSpec(memory_space=VMEM),
        scratch_shapes=[
            pltpu.VMEM((RING, PIECE, width), BF16),
            pltpu.SemaphoreType.DMA((RING,)),
        ],
        compiler_params=pltpu.CompilerParams(vmem_limit_bytes=26 * 2**20),
        cost_estimate=cost(bytes_accessed),
        name="partials",
    )


STEPS = 2
ROWS = 16


def outer_made_first(n, k):
    early = place(n) < n // 2
    return early if k == 1 else jnp.logical_not(early)


def next_kernel(chunk, n, s, flow, keys, *refs):
    sums, (came, out) = dict(zip(keys, refs)), refs[len(keys) :]
    k = s if flow == 0 else n - s
    mine = place(n) if flow == 0 else n - 1 - place(n)
    rows = came.shape[0]

    @pl.when((mine >= s) & (mine < n - 1))
    def _():
        out[...] = came[...]

    def add(held):
        def one(i, carry):
            start = pl.multiple_of(i * ROWS, ROWS)
            old = decoder(chunk, came, start, ROWS)

            def value(column):
                return held[0, pl.ds(start, ROWS), column : column + LANES] + old(column)

            encode(chunk, value, out, start, ROWS)
            return carry

        lax.fori_loop(0, rows // ROWS, one, 0)

    if ("second", 0) not in sums:

        @pl.when(mine < s)
        def _():
            add(sums[keys[0]])

    else:

        @pl.when((mine < s) & outer_made_first(n, k))
        def _():
            add(sums["first", 0])

        @pl.when((mine < s) & jnp.logical_not(outer_made_first(n, k)))
        def _():
            add(sums["second", 0])


def next_message(chunk, n, s, flow, first, second, came, deps=()):
    rows = came.shape[0]
    step = rows // STEPS
    k = s if flow == 0 else n - s
    keys = [("first", 0) if k in (1, n - 1) else ("second", k)]
    if s == n - 1 and s > 1:
        keys.append(("second", 0))
    message = pl.BlockSpec((step, chunk.message), lambda i: (i, 0))
    return call(
        functools.partial(next_kernel, chunk, n, s, flow, keys),
        [first if which == "first" else second for which, _ in keys] + [came],
        [pl.BlockSpec((1, step, chunk.width), lambda i, at=at: (at, i, 0)) for _, at in keys]
        + [message],
        deps,
        grid=(STEPS,),
        out_shape=jax.ShapeDtypeStruct(came.shape, I16),
        out_specs=message,
        compiler_params=params(1, 12),
        cost_estimate=cost(40e6 if s < n - 1 else 1e6 if flow == 0 else 100e6),
        name="next",
    )


def wait_kernel(out):
    out[...] = jnp.zeros(out.shape, F32)


def wait_for(deps):
    return call(
        wait_kernel,
        [],
        [],
        deps,
        out_shape=jax.ShapeDtypeStruct((8, LANES), F32),
        out_specs=pl.BlockSpec(memory_space=VMEM),
        compiler_params=pltpu.CompilerParams(vmem_limit_bytes=2**20),
        cost_estimate=cost(40e6),
        name="wait",
    )


def finish_kernel(chunks, at, *refs):
    count = len(chunks)
    sums, rights, lefts = refs[:count], refs[count : 2 * count], refs[2 * count : 3 * count]
    outs = refs[3 * count :]
    rows = rights[0].shape[0]
    for start in range(0, rows, ROWS):
        for chunk, total, right, left in zip(chunks, sums, rights, lefts):
            old_right = decoder(chunk, right, start, ROWS)
            old_left = decoder(chunk, left, start, ROWS)
            for column, which, place in chunk.places():
                value = total[0, start : start + ROWS, column : column + LANES]
                value = value + old_right(column) + old_left(column)
                outs[which][0, start : start + ROWS, place : place + LANES] = value.astype(BF16)


def finish(chunks, sums, at, rights, lefts, examples, widths, deps=()):
    rows = sums[0].shape[1]
    local = rows // examples
    half = local // 2
    return call(
        functools.partial(finish_kernel, chunks, at),
        [*sums, *rights, *lefts],
        [pl.BlockSpec((1, half, x.shape[2]), lambda i: (at, i, 0)) for x in sums]
        + [pl.BlockSpec((half, x.shape[1]), lambda i: (i, 0)) for x in (*rights, *lefts)],
        deps,
        grid=(2 * examples,),
        out_shape=[jax.ShapeDtypeStruct((examples, local, w), BF16) for w in widths],
        out_specs=[pl.BlockSpec((1, half, w), lambda i: (i // 2, i % 2, 0)) for w in widths],
        compiler_params=params(1, 12),
        cost_estimate=cost(1e6),
        name="finish",
    )


NT = (((1,), (1,)), ((), ()))


def gram_kernel(m_ref, out, mine):
    core = lax.axis_index("row") % 2
    for b in range(out.shape[0]):
        masked = m_ref[:, b].reshape(out.shape[1], m_ref.shape[-1])
        out[b] = lax.dot_general(masked, masked, NT, preferred_element_type=F32)

        @pl.when(core == b % 2)
        def _():
            mine[b // 2] = out[b]


def gram(masked, deps=()):
    col_count, examples, local, width = masked.shape
    length = col_count * local
    return call(
        gram_kernel,
        (masked,),
        [pl.BlockSpec(memory_space=VMEM)],
        deps,
        out_shape=[
            jax.ShapeDtypeStruct((count, length, length), F32) for count in (examples, examples // 2)
        ],
        out_specs=[pl.BlockSpec(memory_space=VMEM)] * 2,
        compiler_params=pltpu.CompilerParams(vmem_limit_bytes=16 * 2**20),
        cost_estimate=cost(20e6),
        name="gram",
    )


def take(chunk, message, put, examples, local):
    for b in range(examples):

        def one(i, carry):
            start = pl.multiple_of(i * ROWS, ROWS)
            value = decoder(chunk, message, b * local + start, ROWS)
            for column in range(0, chunk.width, LANES):
                put(b, start, column, value(column).astype(BF16))
            return carry

        lax.fori_loop(0, local // ROWS, one, 0)


def turned(x, shift):
    x = jnp.concatenate([x[-shift:], x[:-shift]], axis=0)
    return pltpu.roll(x, shift, 1)


def mirrored(x, local, first):
    order = [(first - j) % 4 * local for j in range(4)]
    x = jnp.concatenate([x[at : at + local] for at in order], axis=0)
    halves = [pltpu.roll(h, local, 1) for h in (x[:, : 2 * local], x[:, 2 * local :])]
    return jnp.concatenate(halves if first == 1 else halves[::-1], axis=1)


def join_kernel(chunk, n, slots, early, gram_ref, came, came_to_other, hidden, context, *refs):
    firsts, seconds = refs[:slots], refs[slots : 2 * slots]
    joined, out = refs[-2:]
    p = place(n)
    arrays = (hidden, context)
    examples, local, _ = hidden.shape
    for column, which, at in chunk.places():
        joined[:, :local, column : column + LANES] = arrays[which][:, :, at : at + LANES]

    for k in range(1, n):

        def put(b, row, column, value):
            joined[b, pl.ds(k * local + row, ROWS), column : column + LANES] = value

        if k - 1 < slots:

            @pl.when(p >= k)
            def _():
                take(chunk, firsts[k - 1], put, examples, local)

        if n - k - 1 < slots:

            @pl.when(p < k)
            def _():
                take(chunk, seconds[n - k - 1], put, examples, local)

    lane = lax.broadcasted_iota(jnp.int32, out.shape, 1)
    out[...] = jnp.zeros(out.shape, F32)

    def norm(came_from):
        total = jnp.zeros(out.shape, F32)
        for b in range(examples):
            feature = joined[b]
            feature_gram = lax.dot_general(feature, feature, NT, preferred_element_type=F32)
            masked_gram = gram_ref[b]
            if came_from:
                shift, first = (local, 1) if came_from == 1 else ((n - 1) * local, 3)
                mine = turned(came[b // 2], shift)
                others = mirrored(came_to_other[b // 2], local, first)
                masked_gram += jnp.where(lax.axis_index("row") % 2 == b % 2, mine, others)
            total = jnp.where(lane == b, jnp.sum(feature_gram * masked_gram), total)
        out[...] = total

    if early:
        pl.when(p == 1)(lambda: norm(1))
        pl.when(p == 2)(lambda: norm(2))
    else:
        norm(0)


def join(chunk, n, early, grams, hidden, context, firsts, seconds, deps=()):
    examples, local, _ = hidden.shape
    arrays = [*grams, hidden, context, *firsts, *seconds]
    shape = (examples, n * local, chunk.width)
    return call(
        functools.partial(join_kernel, chunk, n, len(firsts), early),
        arrays,
        [pl.BlockSpec(memory_space=VMEM)] * len(arrays),
        deps,
        out_shape=[jax.ShapeDtypeStruct(shape, BF16), jax.ShapeDtypeStruct((8, LANES), F32)],
        out_specs=[pl.BlockSpec(memory_space=VMEM)] * 2,
        compiler_params=pltpu.CompilerParams(vmem_limit_bytes=32 * 2**20),
        cost_estimate=cost(1e6),
        name="join",
    )


def sum_over(x, axis, count, groups):
    for group in groups:
        came = [lax.ppermute(x, axis, [(i, i ^ j) for i in range(count)]) for j in group]
        came = lax.optimization_barrier(came)
        for y in came:
            x = x + y
    return x


def weight_kernel(chunk, widths, n, factor, m_ref, joined, *refs):
    last, (token, *outs), (features, message, sems) = refs[:-6], refs[-6:-3], refs[-3:]
    examples, length = features.shape[:2]
    local = length // n
    p = place(n)

    @pl.when(pl.program_id(0) == 0)
    def _():
        copies = [
            pltpu.make_async_copy(joined.at[b], features.at[b], sems.at[b]) for b in range(examples)
        ]

        def fill(source, k):
            came = pltpu.make_async_copy(source, message, sems.at[examples])
            came.start()
            came.wait()

            def put(b, row, column, value):
                features[b, pl.ds(k * local + row, ROWS), column : column + LANES] = value

            take(chunk, message, put, examples, local)

        for copy in copies:
            copy.start()
        for copy in copies:
            copy.wait()
        if last:
            pl.when(p == 0)(lambda: fill(last[1], 1))
            pl.when(p == n - 1)(lambda: fill(last[0], n - 1))
        token[...] = jnp.zeros(token.shape, F32)

    masked = [m_ref[:, b].reshape(length, m_ref.shape[-1]) for b in range(examples)]
    for column in range(0, sum(widths), LANES):
        out, at = (0, column) if column < widths[0] else (1, column - widths[0])
        total = None
        for b in range(examples):
            each = lax.dot_general(
                features[b, :, column : column + LANES],
                masked[b],
                (((0,), (0,)), ((), ())),
                preferred_element_type=F32,
            )
            each = factor[out, b] * each
            total = each if total is None else total + each
        outs[out][at : at + LANES] = total


def weight_grads(chunk, factor, masked, joined, last, widths, deps=()):
    n, examples, local, width = masked.shape
    tile = min(256, width)
    anywhere = pl.BlockSpec(memory_space=pl.ANY)
    return call(
        functools.partial(weight_kernel, chunk, widths, n),
        [factor, masked, joined, *last],
        [
            pl.BlockSpec(memory_space=pltpu.SMEM),
            pl.BlockSpec((n, examples, local, tile), lambda i: (0, 0, 0, i)),
        ]
        + [anywhere] * (1 + len(last)),
        deps,
        grid=(width // tile,),
        out_shape=[jax.ShapeDtypeStruct((8, LANES), F32)]
        + [jax.ShapeDtypeStruct((w, width), F32) for w in widths],
        out_specs=[full((8, LANES))] + [pl.BlockSpec((w, tile), lambda i: (0, i)) for w in widths],
        scratch_shapes=[
            pltpu.VMEM(joined.shape, BF16),
            pltpu.VMEM((examples * local, chunk.message), I16),
            pltpu.SemaphoreType.DMA((examples + 1,)),
        ],
        compiler_params=params(1, 26),
        cost_estimate=cost(1e6),
        name="weights",
    )


def body(row_count, col_count, scales, cotangent, hidden, context, wa, wb, spans):
    n = col_count
    widths = (hidden.shape[2], context.shape[2])
    examples = hidden.shape[0]
    chunk = Chunk([(0, 0, widths[0]), (1, 0, widths[1])])

    def send(x, flow):
        return lax.ppermute(x, ("row", "col"), flow_pairs(n, row_count, flow))

    own = code_own(chunk, hidden, context)
    came = [[send(own, 0)], [send(own, 1)]]
    masked = arrange(gather_rows(cotangent, row_count, (own,)), spans, row_count, n)

    early = n == 4
    inward = [(row * n + a, row * n + b) for row in range(row_count) for a, b in ((0, 1), (3, 2))]
    cores = [(i, i ^ 1) for i in range(row_count)]

    def factors(sq_norm):
        sq_norm = sum_over(sq_norm, "row", row_count, [[1], range(2, row_count, 2)])
        sq_norm = sum_over(sq_norm, "col", n, [range(1, n)])
        factor = 1.0 / (jnp.sqrt(sq_norm[0, :examples]) + GAMMA)
        return jnp.stack([factor * scale for scale in scales])

    first_ks = [lambda p: jnp.where(p < n // 2, 1, n - 1)]
    second_ks = [lambda p: jnp.where(p < n // 2, n - 1, 1), lambda p: 0]
    second_ks += [lambda p, k=k: k for k in range(2, n - 1)]
    first = partials(chunk, masked, first_ks, wa, wb, 4e6)
    second, latest = first, ()
    for s in range(1, n):
        if s == n - 1 and early:
            joined, sq_norm = join(
                chunk, n, True, grams, hidden, context, came[0][:2], came[1][:2], latest
            )
            factor = factors(sq_norm)
            latest = (factor,)
        for flow in (0, 1):
            message = next_message(chunk, n, s, flow, first, second, came[flow][-1], latest)
            latest = (message,)
            came[flow].append(send(message, flow))
            if s == 1 and flow == 0:
                masked_gram, mine = gram(masked, latest)
                grams = [masked_gram, mine, mine]
                if early:
                    grams[1] = lax.ppermute(mine, ("row", "col"), inward)
                latest = (masked_gram,)
            if s == 2 and flow == 0 and early:
                grams[2] = lax.ppermute(after(grams[1], message), "row", cores)
        if s == 1:
            second = partials(chunk, masked, second_ks, wa, wb, 4e6, latest)
            latest = (second,)

    if early:
        last = [came[0][2], came[1][2]]
    else:
        last = []
        joined, sq_norm = join(
            chunk, n, False, grams, hidden, context, came[0][:-1], came[1][:-1], latest
        )
        factor = factors(sq_norm)
    token, down_grad, heads_grad = weight_grads(
        chunk, factor, masked, joined, last, widths, latest
    )
    token = wait_for((came[0][-1], token))
    hidden_grad, context_grad = finish(
        [chunk], [second], 1, [came[0][-1]], [came[1][-1]], examples, widths, (token,)
    )
    return down_grad, heads_grad, hidden_grad, context_grad


def solution(mesh):
    row_count, col_count = mesh.shape["row"], mesh.shape["col"]

    def run(cotangent, hidden, context, down_weight, heads_weight, spans):
        examples = hidden.shape[0]
        scales = tuple(math.sqrt(w.shape[0] * w.shape[1]) / examples for w in (down_weight, heads_weight))
        in_specs = (
            P(None, "row", "col"),
            P(None, "col", "row"),
            P(None, "col", "row"),
            P("row", "col"),
            P("row", "col"),
            P(),
        )
        out_specs = (P("row", "col"), P("row", "col"), P(None, "col", "row"), P(None, "col", "row"))
        return jax.shard_map(
            functools.partial(body, row_count, col_count, scales),
            mesh=mesh,
            in_specs=in_specs,
            out_specs=out_specs,
            check_vma=False,
        )(cotangent, hidden, context, down_weight, heads_weight, spans)

    return run
```

```python
import functools
import math

import jax
import jax.numpy as jnp
from jax import lax
from jax.experimental import pallas as pl
from jax.experimental.pallas import tpu as pltpu
from jax.sharding import PartitionSpec as P

GAMMA = 0.01
VMEM = pltpu.VMEM
F32 = jnp.float32
BF16 = jnp.bfloat16
I16 = jnp.int16
LANES = 128


def params(grid_dims, mebibytes):
    return pltpu.CompilerParams(
        dimension_semantics=("arbitrary",) * grid_dims, vmem_limit_bytes=mebibytes * 2**20
    )


def cost(bytes_accessed):
    return pl.CostEstimate(flops=int(300 * bytes_accessed), bytes_accessed=int(bytes_accessed), transcendentals=0)


def held_back(kernel, count):
    def run(*refs, operands):
        kernel(*refs[: operands - count], *refs[operands:])

    return run


def call(kernel, arrays, specs, deps=(), **rest):
    operands = len(arrays) + len(deps)
    if deps:
        kernel = functools.partial(held_back(kernel, len(deps)), operands=operands)
    specs = list(specs) + [pl.BlockSpec(memory_space=pl.ANY)] * len(deps)
    return pl.pallas_call(kernel, in_specs=specs, **rest)(*arrays, *deps)


def full(shape):
    return pl.BlockSpec(shape, lambda *_: (0,) * len(shape))


class Chunk:
    def __init__(self, parts):
        self.parts = parts
        self.width = sum(p[2] for p in parts)
        self.groups = []
        column = 0
        for _, _, size in parts:
            count = -(-size // 1024)
            tiles = size // LANES
            for g in range(count):
                begin, end = tiles * g // count, tiles * (g + 1) // count
                self.groups.append((column + begin * LANES, (end - begin) * LANES))
            column += size
        self.message = self.width + LANES

    def places(self):
        column = 0
        for which, first, size in self.parts:
            for at in range(0, size, LANES):
                yield column + at, which, first + at
            column += size


TOP = 32760.0


def encode(chunk, value, out, start, rows):
    lane = lax.broadcasted_iota(jnp.int32, (rows, LANES), 1)
    side = jnp.zeros((rows, LANES), F32)
    at = pl.ds(start, rows)
    for g, (first, size) in enumerate(chunk.groups):
        values = [value(column) for column in range(first, first + size, LANES)]
        largest = jnp.abs(values[0])
        for v in values[1:]:
            largest = jnp.maximum(largest, jnp.abs(v))
        largest = jnp.max(largest, axis=1, keepdims=True)
        exponent = jnp.clip(jnp.ceil(jnp.log2(jnp.maximum(largest, 1e-37))), -110.0, 126.0)
        mantissa = jnp.floor(largest * jnp.exp2(-exponent) * 8192.0) + 2.0
        inverse = jnp.broadcast_to((TOP * 8192.0 / mantissa) * jnp.exp2(-exponent), (rows, LANES))
        side = jnp.where(lane == 2 * g, exponent, jnp.where(lane == 2 * g + 1, mantissa, side))
        for n, v in enumerate(values):
            codes = jnp.floor(v * inverse + 0.5).astype(jnp.int32).astype(I16)
            out[at, first + n * LANES : first + (n + 1) * LANES] = codes
    out[at, chunk.width :] = side.astype(jnp.int32).astype(I16)


def decoder(chunk, message, start, rows):
    at = pl.ds(start, rows)
    side = message[at, chunk.width :].astype(jnp.int32).astype(F32)
    scales = []
    for g in range(len(chunk.groups)):
        scale = jnp.exp2(side[:, 2 * g : 2 * g + 1]) * (side[:, 2 * g + 1 : 2 * g + 2] / (TOP * 8192.0))
        scales.append(jnp.broadcast_to(scale, (rows, LANES)))

    def value(column):
        g = [i for i, (first, size) in enumerate(chunk.groups) if first <= column < first + size][0]
        return message[at, column : column + LANES].astype(jnp.int32).astype(F32) * scales[g]

    return value


def code_kernel(chunk, step, hidden, context, out):
    arrays = (hidden, context)
    places = {column: (which, at) for column, which, at in chunk.places()}
    local = hidden.shape[1]
    for b in range(hidden.shape[0]):
        for start in range(0, local, step):

            def value(column):
                which, at = places[column]
                return arrays[which][b, start : start + step, at : at + LANES].astype(F32)

            encode(chunk, value, out, b * local + start, step)


def code_own(chunk, hidden, context, deps=()):
    examples, local, _ = hidden.shape
    rows = examples * local
    return call(
        functools.partial(code_kernel, chunk, 16),
        (hidden, context),
        [pl.BlockSpec(memory_space=VMEM)] * 2,
        deps,
        out_shape=jax.ShapeDtypeStruct((rows, chunk.message), I16),
        out_specs=pl.BlockSpec(memory_space=VMEM),
        compiler_params=pltpu.CompilerParams(vmem_limit_bytes=16 * 2**20),
        cost_estimate=cost(20e6),
        name="code",
    )


def place(n):
    c = lax.axis_index("col")
    return jnp.where(lax.axis_index("row") % 2 == 0, c, n - 1 - c)


def flow_pairs(n, row_count, flow):
    pairs = []
    for row in range(row_count):
        for c in range(n - 1):
            low, high = row * n + c, row * n + c + 1
            pairs.append((low, high) if (row % 2 == 0) == (flow == 0) else (high, low))
    return pairs


def arrange_kernel(row_count, col_count, spans, *refs):
    pieces, out = refs[:-1], refs[-1]
    r, c = lax.axis_index("row"), lax.axis_index("col")
    examples, held, _ = pieces[0].shape
    per_block = row_count // col_count
    for j, piece in enumerate(pieces):
        source = r ^ j
        block = source // per_block
        k = jnp.where(r % 2 == 0, c - block, block - c)
        k = lax.rem(k + col_count, col_count)
        start = pl.multiple_of(lax.rem(source, per_block) * held, held)
        position = source * held + lax.broadcasted_iota(jnp.int32, (held, 1), 0)
        for b in range(examples):
            keep = (position >= spans[b, 0]) & (position < spans[b, 1])
            value = piece[b].astype(F32) * keep.astype(F32)
            out[k, b, pl.ds(start, held), :] = value.astype(BF16)


def arrange(pieces, spans, row_count, col_count):
    examples, held, width = pieces[0].shape
    local = held * row_count // col_count
    shape = (col_count, examples, local, width)
    return pl.pallas_call(
        functools.partial(arrange_kernel, row_count, col_count),
        out_shape=jax.ShapeDtypeStruct(shape, BF16),
        in_specs=[pl.BlockSpec(memory_space=pltpu.SMEM)]
        + [pl.BlockSpec(memory_space=VMEM)] * len(pieces),
        out_specs=pl.BlockSpec(memory_space=VMEM),
        compiler_params=pltpu.CompilerParams(vmem_limit_bytes=12 * 2**20),
        cost_estimate=cost(20e6),
        name="arrange",
    )(spans, *pieces)


def after(x, *others):
    return lax.optimization_barrier((x, *others))[0]


def after(x, *others):
    return lax.optimization_barrier((x, *others))[0]


def gather_rows(x, row_count, others):
    near = [x]
    for j in range(2, row_count, 2):
        near.append(lax.ppermute(x, "row", [(i, i ^ j) for i in range(row_count)]))
    pieces = []
    for j, piece in enumerate(near):
        if j > 0:
            piece = after(piece, *others)
        pieces.append(piece)
        pieces.append(lax.ppermute(piece, "row", [(i, i ^ 1) for i in range(row_count)]))
    return pieces


PIECE = 512
RING = 4


def pieces_of(size):
    return [(start, min(PIECE, size - start)) for start in range(0, size, PIECE)]


def partial_kernel(plan, ks, m_ref, wa, wb, out, held, sems):
    weights = (wa, wb)

    def copy(number):
        which, source, _, size = plan[number]
        slot = number % RING
        return pltpu.make_async_copy(
            weights[which].at[pl.ds(source, size)], held.at[slot, pl.ds(0, size)], sems.at[slot]
        )

    for number in range(min(RING, len(plan))):
        copy(number).start()
    rows = out.shape[1]
    p = place(m_ref.shape[0])
    masked = jnp.concatenate(
        [m_ref[pl.ds(k(p), 1)].reshape(rows, m_ref.shape[-1]) for k in ks], axis=0
    )
    for number, (_, _, start, size) in enumerate(plan):
        copy(number).wait()
        value = lax.dot_general(
            masked, held[number % RING, pl.ds(0, size)], NT, preferred_element_type=F32
        )
        for n in range(len(ks)):
            out[n, :, start : start + size] = value[n * rows : (n + 1) * rows]
        if number + RING < len(plan):
            copy(number + RING).start()


def partials(chunk, masked, ks, wa, wb, bytes_accessed, deps=()):
    _, examples, local, width = masked.shape
    rows = examples * local
    plan, column = [], 0
    for which, first, count in chunk.parts:
        for start, size in pieces_of(count):
            plan.append((which, first + start, column + start, size))
        column += count
    return call(
        functools.partial(partial_kernel, plan, ks),
        (masked, wa, wb),
        [pl.BlockSpec(memory_space=VMEM)] + [pl.BlockSpec(memory_space=pltpu.HBM)] * 2,
        deps,
        out_shape=jax.ShapeDtypeStruct((len(ks), rows, chunk.width), F32),
        out_specs=pl.BlockSpec(memory_space=VMEM),
        scratch_shapes=[
            pltpu.VMEM((RING, PIECE, width), BF16),
            pltpu.SemaphoreType.DMA((RING,)),
        ],
        compiler_params=pltpu.CompilerParams(vmem_limit_bytes=26 * 2**20),
        cost_estimate=cost(bytes_accessed),
        name="partials",
    )


STEPS = 2
ROWS = 16


def outer_made_first(n, k):
    early = place(n) < n // 2
    return early if k == 1 else jnp.logical_not(early)


def next_kernel(chunk, n, s, flow, keys, *refs):
    sums, (came, out) = dict(zip(keys, refs)), refs[len(keys) :]
    k = s if flow == 0 else n - s
    mine = place(n) if flow == 0 else n - 1 - place(n)
    rows = came.shape[0]

    @pl.when((mine >= s) & (mine < n - 1))
    def _():
        out[...] = came[...]

    def add(held):
        def one(i, carry):
            start = pl.multiple_of(i * ROWS, ROWS)
            old = decoder(chunk, came, start, ROWS)

            def value(column):
                return held[0, pl.ds(start, ROWS), column : column + LANES] + old(column)

            encode(chunk, value, out, start, ROWS)
            return carry

        lax.fori_loop(0, rows // ROWS, one, 0)

    if ("second", 0) not in sums:

        @pl.when(mine < s)
        def _():
            add(sums[keys[0]])

    else:

        @pl.when((mine < s) & outer_made_first(n, k))
        def _():
            add(sums["first", 0])

        @pl.when((mine < s) & jnp.logical_not(outer_made_first(n, k)))
        def _():
            add(sums["second", 0])


def next_message(chunk, n, s, flow, first, second, came, deps=()):
    rows = came.shape[0]
    step = rows // STEPS
    k = s if flow == 0 else n - s
    keys = [("first", 0) if k in (1, n - 1) else ("second", k)]
    if s == n - 1 and s > 1:
        keys.append(("second", 0))
    message = pl.BlockSpec((step, chunk.message), lambda i: (i, 0))
    return call(
        functools.partial(next_kernel, chunk, n, s, flow, keys),
        [first if which == "first" else second for which, _ in keys] + [came],
        [pl.BlockSpec((1, step, chunk.width), lambda i, at=at: (at, i, 0)) for _, at in keys]
        + [message],
        deps,
        grid=(STEPS,),
        out_shape=jax.ShapeDtypeStruct(came.shape, I16),
        out_specs=message,
        compiler_params=params(1, 12),
        cost_estimate=cost(40e6 if s < n - 1 else 1e6 if flow == 0 else 100e6),
        name="next",
    )


def wait_kernel(out):
    out[...] = jnp.zeros(out.shape, F32)


def wait_for(deps):
    return call(
        wait_kernel,
        [],
        [],
        deps,
        out_shape=jax.ShapeDtypeStruct((8, LANES), F32),
        out_specs=pl.BlockSpec(memory_space=VMEM),
        compiler_params=pltpu.CompilerParams(vmem_limit_bytes=2**20),
        cost_estimate=cost(40e6),
        name="wait",
    )


def finish_kernel(chunks, at, *refs):
    count = len(chunks)
    sums, rights, lefts = refs[:count], refs[count : 2 * count], refs[2 * count : 3 * count]
    outs = refs[3 * count :]
    rows = rights[0].shape[0]
    for start in range(0, rows, ROWS):
        for chunk, total, right, left in zip(chunks, sums, rights, lefts):
            old_right = decoder(chunk, right, start, ROWS)
            old_left = decoder(chunk, left, start, ROWS)
            for column, which, place in chunk.places():
                value = total[0, start : start + ROWS, column : column + LANES]
                value = value + old_right(column) + old_left(column)
                outs[which][0, start : start + ROWS, place : place + LANES] = value.astype(BF16)


def finish(chunks, sums, at, rights, lefts, examples, widths, deps=()):
    rows = sums[0].shape[1]
    local = rows // examples
    half = local // 2
    return call(
        functools.partial(finish_kernel, chunks, at),
        [*sums, *rights, *lefts],
        [pl.BlockSpec((1, half, x.shape[2]), lambda i: (at, i, 0)) for x in sums]
        + [pl.BlockSpec((half, x.shape[1]), lambda i: (i, 0)) for x in (*rights, *lefts)],
        deps,
        grid=(2 * examples,),
        out_shape=[jax.ShapeDtypeStruct((examples, local, w), BF16) for w in widths],
        out_specs=[pl.BlockSpec((1, half, w), lambda i: (i // 2, i % 2, 0)) for w in widths],
        compiler_params=params(1, 12),
        cost_estimate=cost(1e6),
        name="finish",
    )


NT = (((1,), (1,)), ((), ()))


def gram_kernel(m_ref, out, mine):
    core = lax.axis_index("row") % 2
    for b in range(out.shape[0]):
        masked = m_ref[:, b].reshape(out.shape[1], m_ref.shape[-1])
        out[b] = lax.dot_general(masked, masked, NT, preferred_element_type=F32)

        @pl.when(core == b % 2)
        def _():
            mine[b // 2] = out[b]


def gram(masked, deps=()):
    col_count, examples, local, width = masked.shape
    length = col_count * local
    return call(
        gram_kernel,
        (masked,),
        [pl.BlockSpec(memory_space=VMEM)],
        deps,
        out_shape=[
            jax.ShapeDtypeStruct((count, length, length), F32) for count in (examples, examples // 2)
        ],
        out_specs=[pl.BlockSpec(memory_space=VMEM)] * 2,
        compiler_params=pltpu.CompilerParams(vmem_limit_bytes=16 * 2**20),
        cost_estimate=cost(20e6),
        name="gram",
    )


def take(chunk, message, put, examples, local):
    for b in range(examples):

        def one(i, carry):
            start = pl.multiple_of(i * ROWS, ROWS)
            value = decoder(chunk, message, b * local + start, ROWS)
            for column in range(0, chunk.width, LANES):
                put(b, start, column, value(column).astype(BF16))
            return carry

        lax.fori_loop(0, local // ROWS, one, 0)


def turned(x, shift):
    x = jnp.concatenate([x[-shift:], x[:-shift]], axis=0)
    return pltpu.roll(x, shift, 1)


def mirrored(x, local, first):
    order = [(first - j) % 4 * local for j in range(4)]
    x = jnp.concatenate([x[at : at + local] for at in order], axis=0)
    halves = [pltpu.roll(h, local, 1) for h in (x[:, : 2 * local], x[:, 2 * local :])]
    return jnp.concatenate(halves if first == 1 else halves[::-1], axis=1)


def join_kernel(chunk, n, slots, early, gram_ref, came, came_to_other, hidden, context, *refs):
    firsts, seconds = refs[:slots], refs[slots : 2 * slots]
    joined, out = refs[-2:]
    p = place(n)
    arrays = (hidden, context)
    examples, local, _ = hidden.shape
    for column, which, at in chunk.places():
        joined[:, :local, column : column + LANES] = arrays[which][:, :, at : at + LANES]

    for k in range(1, n):

        def put(b, row, column, value):
            joined[b, pl.ds(k * local + row, ROWS), column : column + LANES] = value

        if k - 1 < slots:

            @pl.when(p >= k)
            def _():
                take(chunk, firsts[k - 1], put, examples, local)

        if n - k - 1 < slots:

            @pl.when(p < k)
            def _():
                take(chunk, seconds[n - k - 1], put, examples, local)

    lane = lax.broadcasted_iota(jnp.int32, out.shape, 1)
    out[...] = jnp.zeros(out.shape, F32)

    def norm(came_from):
        total = jnp.zeros(out.shape, F32)
        for b in range(examples):
            feature = joined[b]
            feature_gram = lax.dot_general(feature, feature, NT, preferred_element_type=F32)
            masked_gram = gram_ref[b]
            if came_from:
                shift, first = (local, 1) if came_from == 1 else ((n - 1) * local, 3)
                mine = turned(came[b // 2], shift)
                others = mirrored(came_to_other[b // 2], local, first)
                masked_gram += jnp.where(lax.axis_index("row") % 2 == b % 2, mine, others)
            total = jnp.where(lane == b, jnp.sum(feature_gram * masked_gram), total)
        out[...] = total

    if early:
        pl.when(p == 1)(lambda: norm(1))
        pl.when(p == 2)(lambda: norm(2))
    else:
        norm(0)


def join(chunk, n, early, grams, hidden, context, firsts, seconds, deps=()):
    examples, local, _ = hidden.shape
    arrays = [*grams, hidden, context, *firsts, *seconds]
    shape = (examples, n * local, chunk.width)
    return call(
        functools.partial(join_kernel, chunk, n, len(firsts), early),
        arrays,
        [pl.BlockSpec(memory_space=VMEM)] * len(arrays),
        deps,
        out_shape=[jax.ShapeDtypeStruct(shape, BF16), jax.ShapeDtypeStruct((8, LANES), F32)],
        out_specs=[pl.BlockSpec(memory_space=VMEM)] * 2,
        compiler_params=pltpu.CompilerParams(vmem_limit_bytes=32 * 2**20),
        cost_estimate=cost(1e6),
        name="join",
    )


def sum_over(x, axis, count, groups):
    for group in groups:
        came = [lax.ppermute(x, axis, [(i, i ^ j) for i in range(count)]) for j in group]
        came = lax.optimization_barrier(came)
        for y in came:
            x = x + y
    return x


def weight_kernel(chunk, widths, n, factor, m_ref, joined, *refs):
    last, (token, *outs), (features, message, sems) = refs[:-6], refs[-6:-3], refs[-3:]
    examples, length = features.shape[:2]
    local = length // n
    p = place(n)

    @pl.when(pl.program_id(0) == 0)
    def _():
        copies = [
            pltpu.make_async_copy(joined.at[b], features.at[b], sems.at[b]) for b in range(examples)
        ]

        def fill(source, k):
            came = pltpu.make_async_copy(source, message, sems.at[examples])
            came.start()
            came.wait()

            def put(b, row, column, value):
                features[b, pl.ds(k * local + row, ROWS), column : column + LANES] = value

            take(chunk, message, put, examples, local)

        for copy in copies:
            copy.start()
        for copy in copies:
            copy.wait()
        if last:
            pl.when(p == 0)(lambda: fill(last[1], 1))
            pl.when(p == n - 1)(lambda: fill(last[0], n - 1))
        token[...] = jnp.zeros(token.shape, F32)

    masked = [m_ref[:, b].reshape(length, m_ref.shape[-1]) for b in range(examples)]
    for column in range(0, sum(widths), LANES):
        out, at = (0, column) if column < widths[0] else (1, column - widths[0])
        total = None
        for b in range(examples):
            each = lax.dot_general(
                features[b, :, column : column + LANES],
                masked[b],
                (((0,), (0,)), ((), ())),
                preferred_element_type=F32,
            )
            each = factor[out, b] * each
            total = each if total is None else total + each
        outs[out][at : at + LANES] = total


def weight_grads(chunk, factor, masked, joined, last, widths, deps=()):
    n, examples, local, width = masked.shape
    tile = min(256, width)
    anywhere = pl.BlockSpec(memory_space=pl.ANY)
    return call(
        functools.partial(weight_kernel, chunk, widths, n),
        [factor, masked, joined, *last],
        [
            pl.BlockSpec(memory_space=pltpu.SMEM),
            pl.BlockSpec((n, examples, local, tile), lambda i: (0, 0, 0, i)),
        ]
        + [anywhere] * (1 + len(last)),
        deps,
        grid=(width // tile,),
        out_shape=[jax.ShapeDtypeStruct((8, LANES), F32)]
        + [jax.ShapeDtypeStruct((w, width), F32) for w in widths],
        out_specs=[full((8, LANES))] + [pl.BlockSpec((w, tile), lambda i: (0, i)) for w in widths],
        scratch_shapes=[
            pltpu.VMEM(joined.shape, BF16),
            pltpu.VMEM((examples * local, chunk.message), I16),
            pltpu.SemaphoreType.DMA((examples + 1,)),
        ],
        compiler_params=params(1, 26),
        cost_estimate=cost(1e6),
        name="weights",
    )


def body(row_count, col_count, scales, cotangent, hidden, context, wa, wb, spans):
    n = col_count
    widths = (hidden.shape[2], context.shape[2])
    examples = hidden.shape[0]
    chunk = Chunk([(0, 0, widths[0]), (1, 0, widths[1])])

    def send(x, flow):
        return lax.ppermute(x, ("row", "col"), flow_pairs(n, row_count, flow))

    own = code_own(chunk, hidden, context)
    came = [[send(own, 0)], [send(own, 1)]]
    masked = arrange(gather_rows(cotangent, row_count, (own,)), spans, row_count, n)

    early = n == 4
    inward = [(row * n + a, row * n + b) for row in range(row_count) for a, b in ((0, 1), (3, 2))]
    cores = [(i, i ^ 1) for i in range(row_count)]

    def over_rows(sq_norm):
        return sum_over(sq_norm, "row", row_count, [[1], range(2, row_count, 2)])

    def factors(sq_norm):
        sq_norm = sum_over(sq_norm, "col", n, [range(1, n)])
        factor = 1.0 / (jnp.sqrt(sq_norm[0, :examples]) + GAMMA)
        return jnp.stack([factor * scale for scale in scales])

    first_ks = [lambda p: jnp.where(p < n // 2, 1, n - 1)]
    second_ks = [lambda p: jnp.where(p < n // 2, n - 1, 1), lambda p: 0]
    second_ks += [lambda p, k=k: k for k in range(2, n - 1)]
    first = partials(chunk, masked, first_ks, wa, wb, 4e6)
    second, latest = first, ()
    for s in range(1, n):
        if s == n - 1 and early:
            joined, sq_norm = join(
                chunk, n, True, grams, hidden, context, came[0][:2], came[1][:2], latest
            )
            sq_norm = over_rows(sq_norm)
            latest = (sq_norm,)
        for flow in (0, 1):
            message = next_message(chunk, n, s, flow, first, second, came[flow][-1], latest)
            latest = (message,)
            came[flow].append(send(message, flow))
            if s == 1 and flow == 0:
                masked_gram, mine = gram(masked, latest)
                grams = [masked_gram, mine, mine]
                if early:
                    grams[1] = lax.ppermute(mine, ("row", "col"), inward)
                latest = (masked_gram,)
            if s == n - 1 and flow == 0 and early:
                factor = factors(after(sq_norm, message))
                latest = (factor,)
            if s == 2 and flow == 0 and early:
                grams[2] = lax.ppermute(after(grams[1], message), "row", cores)
        if s == 1:
            second = partials(chunk, masked, second_ks, wa, wb, 4e6, latest)
            latest = (second,)

    if early:
        last = [came[0][2], came[1][2]]
    else:
        last = []
        joined, sq_norm = join(
            chunk, n, False, grams, hidden, context, came[0][:-1], came[1][:-1], latest
        )
        factor = factors(over_rows(sq_norm))
    token, down_grad, heads_grad = weight_grads(
        chunk, factor, masked, joined, last, widths, latest
    )
    token = wait_for((came[0][-1], token))
    hidden_grad, context_grad = finish(
        [chunk], [second], 1, [came[0][-1]], [came[1][-1]], examples, widths, (token,)
    )
    return down_grad, heads_grad, hidden_grad, context_grad


def solution(mesh):
    row_count, col_count = mesh.shape["row"], mesh.shape["col"]

    def run(cotangent, hidden, context, down_weight, heads_weight, spans):
        examples = hidden.shape[0]
        scales = tuple(math.sqrt(w.shape[0] * w.shape[1]) / examples for w in (down_weight, heads_weight))
        in_specs = (
            P(None, "row", "col"),
            P(None, "col", "row"),
            P(None, "col", "row"),
            P("row", "col"),
            P("row", "col"),
            P(),
        )
        out_specs = (P("row", "col"), P("row", "col"), P(None, "col", "row"), P(None, "col", "row"))
        return jax.shard_map(
            functools.partial(body, row_count, col_count, scales),
            mesh=mesh,
            in_specs=in_specs,
            out_specs=out_specs,
            check_vma=False,
        )(cotangent, hidden, context, down_weight, heads_weight, spans)

    return run
```
